128 devices in a mesh: dp: 16 (over x, z), col: 8 (over y, core).
Axes of the slice: x: 4, y: 4, z: 4, core: 2. Of those that a mesh axis runs over, the one named last changes fastest.
Arguments:
- coefficients: bfloat16 [16, 65536], P(None, 'dp'), may hold values from -0.3125 to 0.3125
- arc_pairs: int32 [2, 65536], P(None, 'dp'), may hold values from 0 to 31, as said below
- live_rows: int32 [16], P('dp'), may hold values from 1 to 4096, 32768 in all
- shared_rows: bfloat16 [65536, 16384], P('dp', 'col'), may hold values from -6 to 6
- prior_panel: float32 [256, 256], replicated, as said below
- prior_shared: float32 [256, 16384], P(None, 'col'), may hold values from -4 to 4
Outputs:
- new_panel: float32 [256, 256], replicated
- new_shared: float32 [256, 16384], P(None, 'col')
The draws below stay inside these ranges and needn't reach their ends.
Inputs may be any that keep to these rules, and one draw needn't show every extreme that they name: `arc_pairs`: the two arcs of a row differ. `prior_panel`: upper triangular with a positive diagonal.
All inputs are finite; a program needn't handle non-finite values. No bound on the sum of `live_rows` on one device may be relied on, other than what follows from the above.
Results may differ from the reference program's by a relative error of at most 0.0003.
Values sent between devices are 32-bit elements; how exact they have to be, the bound alone decides.
A program may use at most 64 MiB of HBM per device.

```python
import math
import jax
import jax.numpy as jnp
import numpy as np
from jax import lax

ARCS = 32
ARC_PAR = 8
PANEL = 256
SHARED = 16384
ROWS_DEV = 4096
ROWS = 65536
N_DP = 16


def draw_arc_pairs(key, part):
    key = jax.random.fold_in(key, 11)
    key_first, key_second = jax.random.split(key)
    first_arc = jax.random.randint(key_first, (ROWS,), 0, ARCS)
    offset_arc = jax.random.randint(key_second, (ROWS,), 1, ARCS)
    second_arc = (first_arc + offset_arc) % ARCS
    return jnp.stack([first_arc, second_arc]).astype(jnp.int32)


def draw_prior_panel(key, part):
    key = jax.random.fold_in(key, 23)
    key_first, key_second = jax.random.split(key)
    diagonal = jax.random.uniform(key_first, (PANEL,), jnp.float32, 0.5, 1.5)
    upper_part = 0.15 * jax.random.normal(key_second, (PANEL, PANEL), jnp.float32)
    triangle = jnp.triu(upper_part, 1) + jnp.diag(diagonal)
    return triangle.astype(jnp.float32)


def steps_of(key, extent, cuts, smallest, high):
    loudness, own = 1.0, jax.random.fold_in(key, 6)
    for axis_at, blocks in cuts:
        steps = jnp.exp(jax.random.uniform(jax.random.fold_in(own, axis_at), (blocks,), jnp.float32, smallest / len(cuts), high / len(cuts)))
        loudness = loudness * jnp.repeat(steps, extent[axis_at] // blocks).reshape([-1 if axis == axis_at else 1 for axis in range(len(extent))])
    return loudness


def profile(count, total, bound, slope):
    loads = [(1 << 20) // math.isqrt(grade ** slope) + 1 for grade in range(2, count + 1)]
    rest, counts = total - bound - (count - 1), [1] * (count - 1)
    while rest > 0:
        movable = [i for i in range(count - 1) if counts[i] < bound]
        mass, left = sum([loads[i] for i in movable]), rest
        for i in movable:
            addition = min(bound - counts[i], max(1, left * loads[i] // mass), rest)
            counts[i] = counts[i] + addition
            rest = rest - addition
    return np.array([bound] + counts)


def uneven(key, count, total, reach, skew):
    if count == 2:
        one = jax.random.randint(key, (), max(1, total - reach), min(reach, total - 1) + 1)
        return jnp.stack([one, total - one])
    tallies = jnp.asarray(profile(count, total, reach, skew), jnp.int32)
    couples = (count - 1) // 2
    donor, taker = tallies[1:1 + 2 * couples:2], tallies[2:2 + 2 * couples:2]
    slack = jnp.minimum(donor - 1, reach - taker)
    shifted = jax.random.randint(jax.random.fold_in(key, 1), (couples,), 0, 1 << 20) % (slack + 1)
    tallies = tallies.at[1:1 + 2 * couples:2].set(donor - shifted).at[2:2 + 2 * couples:2].set(taker + shifted)
    return tallies[jax.random.permutation(jax.random.fold_in(key, 2), count)]


def scatter_about(rng, extent, spread, bound, cuts=(), held_as=jnp.bfloat16):
    loudness = steps_of(rng, extent, cuts, -0.22, 0.18) if cuts else 1.0
    entries = jax.random.normal(rng, extent, jnp.float32) * spread * loudness
    return jnp.minimum(jnp.maximum(entries, -bound), bound).astype(held_as)


def setup_inputs(seed: int = 0) -> dict:
    arg_keys = jax.random.split(jax.random.key(seed), 7)
    return {
        "coefficients": scatter_about(arg_keys[0], (2 * ARC_PAR, ROWS), ((ARCS / (ROWS_DEV * N_DP)) ** 0.5), 0.3125, ((1, 16),)),
        "arc_pairs": draw_arc_pairs(jax.random.fold_in(arg_keys[6], 71), 0),
        "live_rows": uneven(arg_keys[2], N_DP, ROWS_DEV * N_DP // 2, ROWS_DEV, 2).astype(jnp.int32),
        "shared_rows": scatter_about(arg_keys[3], (ROWS, SHARED), 1.0, 6.0, ((0, 16), (1, 8))),
        "prior_panel": draw_prior_panel(jax.random.fold_in(arg_keys[6], 71), 0),
        "prior_shared": scatter_about(arg_keys[5], (PANEL, SHARED), 0.5, 4.0, ((1, 8),), jnp.float32),
    }


def make_panel(coefficients, arc_pairs, live_mask):
    arc_par = coefficients.shape[0] // 2
    panel_width = ARCS * arc_par
    column_arc = jnp.arange(panel_width, dtype=jnp.int32) // arc_par
    first_coef = jnp.tile(coefficients[:arc_par].T, (1, ARCS))
    second_coef = jnp.tile(coefficients[arc_par:].T, (1, ARCS))
    hit_first = arc_pairs[0][:, None] == column_arc[None, :]
    hit_second = arc_pairs[1][:, None] == column_arc[None, :]
    zero_value = jnp.zeros((), coefficients.dtype)
    panel_rows = jnp.where(hit_first, first_coef, zero_value) + jnp.where(hit_second, second_coef, zero_value)
    return jnp.where(live_mask[:, None], panel_rows, zero_value)

def reference(coefficients, arc_pairs, live_rows, shared_rows, prior_panel, prior_shared):
    row_count = coefficients.shape[1]
    row_index = jnp.arange(row_count, dtype=jnp.int32)
    live_mask = row_index % ROWS_DEV < jnp.repeat(live_rows, ROWS_DEV)
    panel_rows = make_panel(coefficients, arc_pairs, live_mask)
    gram = jnp.dot(prior_panel.T, prior_panel, precision=lax.Precision.HIGHEST) + jnp.dot(panel_rows.T.astype(jnp.float32), panel_rows.astype(jnp.float32), preferred_element_type=jnp.float32)

    def add_block(block_index, running):
        offset = (block_index * ROWS_DEV).astype(jnp.int32)
        row_block = lax.dynamic_slice_in_dim(shared_rows, offset, ROWS_DEV, 0)
        own_rows = lax.dynamic_slice_in_dim(panel_rows, offset, ROWS_DEV, 0)
        return running + jnp.dot(own_rows.T.astype(jnp.float32), row_block.astype(jnp.float32), preferred_element_type=jnp.float32)
    cross_data = lax.fori_loop(0, N_DP, add_block, jnp.zeros((PANEL, SHARED), jnp.float32))
    cross = jnp.dot(prior_panel.T, prior_shared, precision=lax.Precision.HIGHEST) + cross_data
    factor_lower = jnp.linalg.cholesky(gram)
    new_shared = lax.linalg.triangular_solve(factor_lower, cross, left_side=True, lower=True)
    return (factor_lower.T, new_shared)
```

```python
import jax
import jax.numpy as jnp
from jax import lax
from jax.experimental import pallas as pl
from jax.experimental.pallas import tpu as pltpu
from jax.sharding import PartitionSpec as P

ARCS = 32
F32 = jnp.float32
BF16 = jnp.bfloat16
HI = lax.Precision.HIGHEST
MESH = pl.DeviceIdType.MESH
SIDE = 4
PANEL = 256
CHUNK = 256
GROUP = PANEL // SIDE
HALF = PANEL // 2


def factor_block(a):
    n = a.shape[0]
    lane = lax.broadcasted_iota(jnp.int32, (n, n), 1)
    row = lax.broadcasted_iota(jnp.int32, (n, n), 0)
    z = jnp.concatenate([a, (lane == row).astype(F32)], axis=1)
    sub = lax.broadcasted_iota(jnp.int32, (8, 2 * n), 0)
    done = []
    for k in range(n // 8):
        m = n - 8 * k
        cols = [jnp.broadcast_to(z[:, 8 * k + j : 8 * k + j + 1], (m, 2 * n)) for j in range(8)]
        rows = lax.broadcasted_iota(jnp.int32, (m, 2 * n), 0)
        pivots = jnp.zeros((8, 2 * n), F32)
        for j in range(8):
            pivot = jnp.broadcast_to(cols[j][j : j + 1, :], (8, 2 * n))
            inverse = 1.0 / pivot
            pivots = jnp.where(sub == j, pivot, pivots)
            scale = jnp.where(rows > j, cols[j] * jnp.broadcast_to(inverse[0:1], (m, 2 * n)), 0.0)
            for i in range(j + 1, 8):
                cols[i] = cols[i] - scale * jnp.broadcast_to(cols[i][j : j + 1, :], (m, 2 * n))
            z = z - scale * jnp.broadcast_to(z[j : j + 1, :], (m, 2 * n))
        done.append(z[:8] * lax.rsqrt(pivots))
        z = z[8:]
    return jnp.concatenate(done, axis=0)


def factor_step(k, z_ref, upper_ref, inverse_ref):
    low, high = 64 * k, 64 * k + 64
    both = factor_block(z_ref[low:high, low:high])
    v = both[:, 64:]
    t = jnp.dot(v, z_ref[low:high, :], precision=HI, preferred_element_type=F32)
    lane = lax.broadcasted_iota(jnp.int32, (64, PANEL), 1)
    row = lax.broadcasted_iota(jnp.int32, (64, PANEL), 0)
    upper_ref[low:high, :] = jnp.where(lane >= low + row, t, 0.0)
    parts = [t[:, :low]] if k else []
    parts.append(v)
    if high < PANEL:
        parts.append(jnp.zeros((64, PANEL - high), F32))
    inverse = jnp.concatenate(parts, axis=1) if len(parts) > 1 else v
    inverse_ref[low:high, :] = inverse
    if high < PANEL:
        update = lax.dot_general(
            t[:, high:],
            jnp.where(lane < high, inverse, t),
            (((0,), (0,)), ((), ())),
            precision=HI,
            preferred_element_type=F32,
        )
        lane = lax.broadcasted_iota(jnp.int32, (PANEL - high, PANEL), 1)
        old = jnp.where((lane >= low) & (lane < high), 0.0, z_ref[high:, :])
        z_ref[high:, :] = old - update


def split2(a):
    first = a.astype(BF16)
    return first, (a - first.astype(F32)).astype(BF16)


def kernel(
    coef_hbm, arcs_hbm, live_ref, shared_hbm, prior_hbm, prior_shared_hbm,
    upper_hbm, out_hbm,
    coef, arcs, prior, prior_cols, panel, shared, prod, opp_in, side_in, total, group_in,
    full, out, gram_part, gram_in, gram_full, z, upper, inverse,
    small_sem, shared_sem, out_sem,
    opp_send, opp_recv, side_send, side_recv, group_send, group_recv,
    gs_send, gs_recv, gp_send, gp_recv, gf_send, gf_recv,
    g1_send, g1_recv, g2_send, g2_recv, g3_send, g3_recv,
):
    dp, col = lax.axis_index("dp"), lax.axis_index("col")
    x, z_at = dp // SIDE, dp % SIDE
    y, core = col // 2, col % 2

    def device(dx=0, dz=0, dy=0, dc=0):
        return (
            (x + dx) % SIDE * SIDE + (z_at + dz) % SIDE,
            (y + dy) % SIDE * 2 + (core + dc) % 2,
        )

    def along(half, d):
        return device(dx=d) if half == 0 else device(dz=d)

    def across(half, d):
        return device(dz=d) if half == 0 else device(dx=d)

    first_at = (x, z_at)
    second_at = (z_at, x)

    barrier = pltpu.get_barrier_semaphore()
    for d in (1, 2, 3):
        pl.semaphore_signal(barrier, inc=1, device_id=device(dx=d), device_id_type=MESH)
        pl.semaphore_signal(barrier, inc=1, device_id=device(dz=d), device_id_type=MESH)
    for dy in range(SIDE):
        for dc in range(2):
            if dy or dc:
                pl.semaphore_signal(
                    barrier, inc=1, device_id=device(dy=dy, dc=dc), device_id_type=MESH
                )

    loads = [
        pltpu.make_async_copy(arcs_hbm, arcs, small_sem.at[0]),
        pltpu.make_async_copy(coef_hbm, coef, small_sem.at[1]),
        pltpu.make_async_copy(prior_hbm, prior, small_sem.at[2]),
    ]
    for half in range(2):
        start = pl.multiple_of((half * SIDE + first_at[half]) * CHUNK, CHUNK)
        loads.append(
            pltpu.make_async_copy(
                prior_shared_hbm.at[:, pl.ds(start, CHUNK)],
                prior_cols.at[half],
                small_sem.at[3 + half],
            )
        )
    order = [(half, rel) for rel in (2, 1, 3, 0) for half in range(2)]
    shared_loads = []
    for half, rel in order:
        start = pl.multiple_of((half * SIDE + (first_at[half] + rel) % SIDE) * CHUNK, CHUNK)
        shared_loads.append(
            pltpu.make_async_copy(
                shared_hbm.at[:, pl.ds(start, CHUNK)],
                shared.at[half * SIDE + rel],
                shared_sem.at[half * SIDE + rel],
            )
        )
    loads[0].start()
    loads[1].start()
    shared_loads[0].start()
    shared_loads[1].start()
    shared_loads[2].start()

    rows = arcs.shape[1]
    loads[0].wait()
    loads[1].wait()
    live = live_ref[0]
    step = 512

    def build(i, carry):
        at = pl.ds(pl.multiple_of(i * step, step), step)
        pair = arcs[:, at]
        row = i * step + lax.broadcasted_iota(jnp.int32, (8, step), 1)
        inside = row < live
        one = jnp.where(inside, jnp.broadcast_to(pair[0:1], (8, step)), -1)
        two = jnp.where(inside, jnp.broadcast_to(pair[1:2], (8, step)), -1)
        values = coef[:, at].astype(F32)
        upper_values, lower_values = values[:8], values[8:]
        for a in range(0, ARCS, 2):
            tiles = [
                jnp.where(one == b, upper_values, jnp.where(two == b, lower_values, 0.0))
                for b in (a, a + 1)
            ]
            panel[8 * a : 8 * a + 16, at] = jnp.concatenate(tiles, axis=0).astype(BF16)
        return carry

    lax.fori_loop(0, rows // step, build, 0)

    own_rows = pl.ds(pl.multiple_of(col * 32, 32), 32)
    gram_part[0] = lax.dot_general(
        panel[own_rows, :],
        panel[...],
        (((1,), (1,)), ((), ())),
        preferred_element_type=F32,
    )
    pl.semaphore_wait(barrier, 13)

    def remote(src, dst, send, recv, to):
        return pltpu.make_async_remote_copy(
            src_ref=src, dst_ref=dst, send_sem=send, recv_sem=recv, device_id=to, device_id_type=MESH
        )

    def gram_axis(d, second):
        if second:
            return device(dx=d * core, dz=d * (1 - core))
        return device(dx=d * (1 - core), dz=d * core)

    g1 = [
        remote(gram_part.at[0], gram_in.at[d - 1], g1_send.at[d - 1], g1_recv.at[d - 1], gram_axis(d, False))
        for d in (1, 2, 3)
    ]
    g2 = [
        remote(gram_part.at[1], gram_in.at[2 + d], g2_send.at[d - 1], g2_recv.at[d - 1], gram_axis(d, True))
        for d in (1, 2, 3)
    ]
    g3 = []
    for dy in range(SIDE):
        for dc in range(2):
            if dy or dc:
                i = 2 * dy + dc - 1
                g3.append(
                    remote(
                        gram_part.at[2], gram_full.at[own_rows, :], g3_send.at[i], g3_recv.at[i],
                        device(dy=dy, dc=dc),
                    )
                )
    for copy in g1:
        copy.start()

    top, bottom = pl.ds(0, HALF), pl.ds(HALF, HALF)

    def opp_copy(half, side):
        where = top if side == 0 else bottom
        i = 2 * half + side
        return remote(
            prod.at[half * SIDE + 2, where, :], opp_in.at[i], opp_send.at[i], opp_recv.at[i],
            along(half, 1 if side == 0 else 3),
        )

    def side_copy(half, side, part):
        where = top if part == 0 else bottom
        i = 4 * half + 2 * side + part
        return remote(
            prod.at[half * SIDE + (1 if side == 0 else 3), where, :],
            side_in.at[2 * half + side, where, :],
            side_send.at[i], side_recv.at[i],
            along(half, 1 if side == 0 else 3),
        )

    def multiply(i):
        half, rel = order[i]
        at = half * SIDE + rel
        shared_loads[i].wait()
        prod[at] = jnp.dot(panel[...], shared[at], preferred_element_type=F32)

    for i in range(8):
        if i + 3 < 8:
            shared_loads[i + 3].start()
        multiply(i)
        half, rel = order[i]
        if rel == 2:
            opp_copy(half, 0).start()
            opp_copy(half, 1).start()
        elif rel == 1:
            side_copy(half, 0, 1).start()
        elif rel == 3:
            side_copy(half, 1, 0).start()
        if i == 3:
            for load in loads[2:]:
                load.start()
        if i == 5:
            for copy in g1:
                copy.wait_recv()
            gram_part[1] = gram_part[0] + gram_in[0] + gram_in[1] + gram_in[2]
            for copy in g2:
                copy.start()

    for side in range(2):
        for half in range(2):
            opp_copy(half, side).wait_recv()
            at = half * SIDE + (1 if side == 0 else 3)
            where = top if side == 0 else bottom
            prod[at, where, :] += opp_in[2 * half + side]
            side_copy(half, side, side).start()

    for load in loads[2:]:
        load.wait()
    prior_t = prior[...].T
    upper[...] = prior_t
    for half in range(2):
        group = pl.ds(pl.multiple_of(second_at[half] * GROUP, GROUP), GROUP)
        full[half * SIDE + first_at[half], group, :] = jnp.dot(
            upper[group, :], prior_cols[half], precision=HI, preferred_element_type=F32
        )
    z[...] = jnp.dot(prior_t, prior[...], precision=HI, preferred_element_type=F32)

    for copy in g2:
        copy.wait_recv()
    gram_part[2] = gram_part[1] + gram_in[3] + gram_in[4] + gram_in[5]
    for copy in g3:
        copy.start()
    gram_full[own_rows, :] = gram_part[2]

    def group_copy(half, d):
        i = 3 * half + d - 1
        group = pl.ds(pl.multiple_of((second_at[half] + d) % SIDE * GROUP, GROUP), GROUP)
        return remote(
            total.at[half, group, :], group_in.at[i], group_send.at[i], group_recv.at[i],
            across(half, d),
        )

    for half in range(2):
        for part in range(2):
            where = top if part == 0 else bottom
            side_copy(half, 0, part).wait_recv()
            side_copy(half, 1, part).wait_recv()
            total[half, where, :] = (
                prod[half * SIDE, where, :]
                + side_in[2 * half, where, :]
                + side_in[2 * half + 1, where, :]
            )
        for d in (2, 1, 3):
            group_copy(half, d).start()

    for copy in g3:
        copy.wait_recv()
    z[...] += gram_full[...]
    factor_step(0, z, upper, inverse)

    def own_copy(half, d):
        i = 3 * half + d - 1
        here = full.at[
            half * SIDE + first_at[half],
            pl.ds(pl.multiple_of(second_at[half] * GROUP, GROUP), GROUP),
            :,
        ]
        return remote(here, here, gs_send.at[i], gs_recv.at[i], across(half, d))

    def chunk_copy(half, d, side):
        i = 8 * half + 2 * d + side
        here = full.at[
            half * SIDE + first_at[half],
            pl.ds(pl.multiple_of((second_at[half] + SIDE - d) % SIDE * GROUP, GROUP), GROUP),
            :,
        ]
        return remote(here, here, gp_send.at[i], gp_recv.at[i], along(half, 1 if side == 0 else 3))

    def forward_copy(half, d, side):
        i = 8 * half + 2 * d + side
        start = (second_at[half] + SIDE - d) % SIDE * GROUP + side * (GROUP // 2)
        here = full.at[
            half * SIDE + (first_at[half] + (3 if side == 0 else 1)) % SIDE,
            pl.ds(pl.multiple_of(start, GROUP // 2), GROUP // 2),
            :,
        ]
        return remote(here, here, gf_send.at[i], gf_recv.at[i], along(half, 1 if side == 0 else 3))

    for half in range(2):
        group = pl.ds(pl.multiple_of(second_at[half] * GROUP, GROUP), GROUP)
        for d in (1, 2, 3):
            group_copy(half, d).wait_recv()
        full[half * SIDE + first_at[half], group, :] += (
            total[half, group, :]
            + group_in[3 * half]
            + group_in[3 * half + 1]
            + group_in[3 * half + 2]
        )
        for d in (2, 1, 3):
            own_copy(half, d).start()
        chunk_copy(half, 0, 0).start()
        chunk_copy(half, 0, 1).start()

    factor_step(1, z, upper, inverse)
    for d in (1, 3, 2):
        for half in range(2):
            own_copy(half, d).wait_recv()
            chunk_copy(half, d, 0).start()
            chunk_copy(half, d, 1).start()
    for half in range(2):
        for side in range(2):
            chunk_copy(half, 0, side).wait_recv()
            forward_copy(half, 0, side).start()
    factor_step(2, z, upper, inverse)
    for d in (1, 3, 2):
        for half in range(2):
            for side in range(2):
                chunk_copy(half, d, side).wait_recv()
                forward_copy(half, d, side).start()
    factor_step(3, z, upper, inverse)
    upper_copy = pltpu.make_async_copy(upper, upper_hbm, out_sem.at[8])
    upper_copy.start()

    w1, w2 = split2(inverse[...])
    weights = jnp.concatenate([w1, w1, w2], axis=1)

    def apply(half, rel):
        at = half * SIDE + (first_at[half] + rel) % SIDE
        a1, a2 = split2(full[at])
        out[half * SIDE + rel] = jnp.dot(
            weights, jnp.concatenate([a1, a2, a1], axis=0), preferred_element_type=F32
        )
        pltpu.make_async_copy(
            out.at[half * SIDE + rel],
            out_hbm.at[:, pl.ds(pl.multiple_of(at * CHUNK, CHUNK), CHUNK)],
            out_sem.at[half * SIDE + rel],
        ).start()

    for rel in (0, 1, 3):
        for half in range(2):
            apply(half, rel)
    for half in range(2):
        for d in range(SIDE):
            for side in range(2):
                forward_copy(half, d, side).wait_recv()
        apply(half, 2)

    for copy in g1 + g2 + g3:
        copy.wait_send()
    for half in range(2):
        for side in range(2):
            opp_copy(half, side).wait_send()
            for part in range(2):
                side_copy(half, side, part).wait_send()
            for d in range(SIDE):
                chunk_copy(half, d, side).wait_send()
                forward_copy(half, d, side).wait_send()
        for d in (1, 2, 3):
            group_copy(half, d).wait_send()
            own_copy(half, d).wait_send()
    upper_copy.wait()
    for half in range(2):
        for rel in range(SIDE):
            at = half * SIDE + (first_at[half] + rel) % SIDE
            pltpu.make_async_copy(
                out.at[half * SIDE + rel],
                out_hbm.at[:, pl.ds(pl.multiple_of(at * CHUNK, CHUNK), CHUNK)],
                out_sem.at[half * SIDE + rel],
            ).wait()


def per_device(coefficients, arc_pairs, live_rows, shared_rows, prior_panel, prior_shared):
    rows, columns = shared_rows.shape
    anywhere = pl.BlockSpec(memory_space=pl.ANY)
    dma = pltpu.SemaphoreType.DMA
    return pl.pallas_call(
        kernel,
        out_shape=[
            jax.ShapeDtypeStruct((PANEL, PANEL), F32),
            jax.ShapeDtypeStruct((PANEL, columns), F32),
        ],
        in_specs=[anywhere, anywhere, pl.BlockSpec(memory_space=pltpu.SMEM)] + [anywhere] * 3,
        out_specs=[anywhere, anywhere],
        scratch_shapes=[
            pltpu.VMEM(coefficients.shape, BF16),
            pltpu.VMEM(arc_pairs.shape, jnp.int32),
            pltpu.VMEM((PANEL, PANEL), F32),
            pltpu.VMEM((2, PANEL, CHUNK), F32),
            pltpu.VMEM((PANEL, rows), BF16),
            pltpu.VMEM((8, rows, CHUNK), BF16),
            pltpu.VMEM((8, PANEL, CHUNK), F32),
            pltpu.VMEM((4, HALF, CHUNK), F32),
            pltpu.VMEM((4, PANEL, CHUNK), F32),
            pltpu.VMEM((2, PANEL, CHUNK), F32),
            pltpu.VMEM((6, GROUP, CHUNK), F32),
            pltpu.VMEM((8, PANEL, CHUNK), F32),
            pltpu.VMEM((8, PANEL, CHUNK), F32),
            pltpu.VMEM((3, 32, PANEL), F32),
            pltpu.VMEM((6, 32, PANEL), F32),
            pltpu.VMEM((PANEL, PANEL), F32),
            pltpu.VMEM((PANEL, PANEL), F32),
            pltpu.VMEM((PANEL, PANEL), F32),
            pltpu.VMEM((PANEL, PANEL), F32),
            dma((5,)), dma((8,)), dma((9,)),
            dma((4,)), dma((4,)), dma((8,)), dma((8,)), dma((6,)), dma((6,)),
            dma((6,)), dma((6,)), dma((16,)), dma((16,)), dma((16,)), dma((16,)),
            dma((3,)), dma((3,)), dma((3,)), dma((3,)), dma((7,)), dma((7,)),
        ],
        compiler_params=pltpu.CompilerParams(
            collective_id=0, has_side_effects=True, vmem_limit_bytes=56 << 20
        ),
    )(coefficients, arc_pairs, live_rows, shared_rows, prior_panel, prior_shared)


def solution(mesh):
    in_specs = (P(None, "dp"), P(None, "dp"), P("dp"), P("dp", "col"), P(), P(None, "col"))
    out_specs = (P(), P(None, "col"))
    return jax.shard_map(
        per_device, mesh=mesh, in_specs=in_specs, out_specs=out_specs, check_vma=False
    )
```

```python
import jax
import jax.numpy as jnp
from jax import lax
from jax.experimental import pallas as pl
from jax.experimental.pallas import tpu as pltpu
from jax.sharding import PartitionSpec as P

ARCS = 32
F32 = jnp.float32
BF16 = jnp.bfloat16
HI = lax.Precision.HIGHEST
MESH = pl.DeviceIdType.MESH
SIDE = 4
PANEL = 256
CHUNK = 256
GROUP = PANEL // SIDE
HALF = PANEL // 2


def factor_pieces(z_ref, upper_ref, inverse_ref):
    n = 64
    sub = lax.broadcasted_iota(jnp.int32, (8, 2 * n), 0)
    for k in range(PANEL // n):
        low, high = n * k, n * k + n
        lane = lax.broadcasted_iota(jnp.int32, (n, n), 1)
        row = lax.broadcasted_iota(jnp.int32, (n, n), 0)
        z = jnp.concatenate([z_ref[low:high, low:high], (lane == row).astype(F32)], axis=1)
        done = []
        for b in range(n // 8):
            m = n - 8 * b
            cols = [jnp.broadcast_to(z[:, 8 * b + j : 8 * b + j + 1], (m, 2 * n)) for j in range(8)]
            rows = lax.broadcasted_iota(jnp.int32, (m, 2 * n), 0)
            pivots = jnp.zeros((8, 2 * n), F32)
            for j in range(8):
                pivot = jnp.broadcast_to(cols[j][j : j + 1, :], (8, 2 * n))
                inverse = 1.0 / pivot
                pivots = jnp.where(sub == j, pivot, pivots)
                scale = jnp.where(
                    rows > j, cols[j] * jnp.broadcast_to(inverse[0:1], (m, 2 * n)), 0.0
                )
                for i in range(j + 1, 8):
                    cols[i] = cols[i] - scale * jnp.broadcast_to(cols[i][j : j + 1, :], (m, 2 * n))
                z = z - scale * jnp.broadcast_to(z[j : j + 1, :], (m, 2 * n))
            done.append(z[:8] * lax.rsqrt(pivots))
            z = z[8:]
            if b % 2 and b < 7:
                yield
        v = jnp.concatenate(done, axis=0)[:, n:]
        t = jnp.dot(v, z_ref[low:high, :], precision=HI, preferred_element_type=F32)
        lane = lax.broadcasted_iota(jnp.int32, (n, PANEL), 1)
        row = lax.broadcasted_iota(jnp.int32, (n, PANEL), 0)
        upper_ref[low:high, :] = jnp.where(lane >= low + row, t, 0.0)
        parts = [t[:, :low]] if k else []
        parts.append(v)
        if high < PANEL:
            parts.append(jnp.zeros((n, PANEL - high), F32))
        inverse = jnp.concatenate(parts, axis=1)
        inverse_ref[low:high, :] = inverse
        yield
        if high < PANEL:
            update = lax.dot_general(
                t[:, high:],
                jnp.where(lane < high, inverse, t),
                (((0,), (0,)), ((), ())),
                precision=HI,
                preferred_element_type=F32,
            )
            lane = lax.broadcasted_iota(jnp.int32, (PANEL - high, PANEL), 1)
            old = jnp.where((lane >= low) & (lane < high), 0.0, z_ref[high:, :])
            z_ref[high:, :] = old - update
            yield


def split2(a):
    first = a.astype(BF16)
    return first, (a - first.astype(F32)).astype(BF16)


def kernel(
    coef_hbm, arcs_hbm, live_hbm, shared_hbm, prior_hbm, prior_shared_hbm,
    upper, inverse, full,
    coef, arcs, live, prior, prior_t, prior_cols, panel, shared, prod, opp_in, side_in, total, group_in,
    gram_part, gram_in, gram_full, z,
    small_sem, shared_sem,
    opp_send, opp_recv, side_send, side_recv, group_send, group_recv,
    gs_send, gs_recv, gp_send, gp_recv, gf_send, gf_recv,
    g1_send, g1_recv, g2_send, g2_recv, g3_send, g3_recv,
):
    dp, col = lax.axis_index("dp"), lax.axis_index("col")
    x, z_at = dp // SIDE, dp % SIDE
    y, core = col // 2, col % 2

    def device(dx=0, dz=0, dy=0, dc=0):
        return (
            (x + dx) % SIDE * SIDE + (z_at + dz) % SIDE,
            (y + dy) % SIDE * 2 + (core + dc) % 2,
        )

    def along(half, d):
        return device(dx=d) if half == 0 else device(dz=d)

    def across(half, d):
        return device(dz=d) if half == 0 else device(dx=d)

    first_at = (x, z_at)
    second_at = (z_at, x)

    barrier = pltpu.get_barrier_semaphore()
    for d in (1, 2, 3):
        pl.semaphore_signal(barrier, inc=1, device_id=device(dx=d), device_id_type=MESH)
        pl.semaphore_signal(barrier, inc=1, device_id=device(dz=d), device_id_type=MESH)
    for dy in range(SIDE):
        for dc in range(2):
            if dy or dc:
                pl.semaphore_signal(
                    barrier, inc=1, device_id=device(dy=dy, dc=dc), device_id_type=MESH
                )

    loads = [
        pltpu.make_async_copy(arcs_hbm, arcs, small_sem.at[0]),
        pltpu.make_async_copy(coef_hbm, coef, small_sem.at[1]),
        pltpu.make_async_copy(live_hbm, live, small_sem.at[2]),
        pltpu.make_async_copy(prior_hbm, prior, small_sem.at[3]),
    ]
    for half in range(2):
        start = pl.multiple_of((half * SIDE + first_at[half]) * CHUNK, CHUNK)
        loads.append(
            pltpu.make_async_copy(
                prior_shared_hbm.at[:, pl.ds(start, CHUNK)],
                prior_cols.at[half],
                small_sem.at[4 + half],
            )
        )
    order = [(half, rel) for rel in (2, 1, 3, 0) for half in range(2)]
    shared_loads = []
    for half, rel in order:
        start = pl.multiple_of((half * SIDE + (first_at[half] + rel) % SIDE) * CHUNK, CHUNK)
        shared_loads.append(
            pltpu.make_async_copy(
                shared_hbm.at[:, pl.ds(start, CHUNK)],
                shared.at[half * SIDE + rel],
                shared_sem.at[half * SIDE + rel],
            )
        )
    for load in loads[:3]:
        load.start()
    shared_loads[0].start()

    rows = arcs.shape[1]
    for load in loads[:3]:
        load.wait()
    live_count = live[0]
    shared_loads[1].start()
    step = 512

    def build(i, carry):
        at = pl.ds(pl.multiple_of(i * step, step), step)
        pair = arcs[:, at]
        row = i * step + lax.broadcasted_iota(jnp.int32, (8, step), 1)
        inside = row < live_count
        one = jnp.where(inside, jnp.broadcast_to(pair[0:1], (8, step)), -1)
        two = jnp.where(inside, jnp.broadcast_to(pair[1:2], (8, step)), -1)
        values = coef[:, at].astype(F32)
        upper_values, lower_values = values[:8], values[8:]
        for a in range(0, ARCS, 2):
            tiles = [
                jnp.where(one == b, upper_values, jnp.where(two == b, lower_values, 0.0))
                for b in (a, a + 1)
            ]
            panel[8 * a : 8 * a + 16, at] = jnp.concatenate(tiles, axis=0).astype(BF16)
        return carry

    lax.fori_loop(0, rows // step, build, 0)
    shared_loads[2].start()

    own_rows = pl.ds(pl.multiple_of(col * 32, 32), 32)

    def remote(src, dst, send, recv, to):
        return pltpu.make_async_remote_copy(
            src_ref=src, dst_ref=dst, send_sem=send, recv_sem=recv, device_id=to, device_id_type=MESH
        )

    def gram_axis(d, second):
        if second:
            return device(dx=d * core, dz=d * (1 - core))
        return device(dx=d * (1 - core), dz=d * core)

    g1 = [
        remote(gram_part.at[0], gram_in.at[d - 1], g1_send.at[d - 1], g1_recv.at[d - 1], gram_axis(d, False))
        for d in (1, 2, 3)
    ]
    g2 = [
        remote(gram_part.at[1], gram_in.at[2 + d], g2_send.at[d - 1], g2_recv.at[d - 1], gram_axis(d, True))
        for d in (1, 2, 3)
    ]
    g3 = []
    for dy in range(SIDE):
        for dc in range(2):
            if dy or dc:
                i = 2 * dy + dc - 1
                g3.append(
                    remote(
                        gram_part.at[2], gram_full.at[own_rows, :], g3_send.at[i], g3_recv.at[i],
                        device(dy=dy, dc=dc),
                    )
                )
    def rows_of(half, e):
        return pl.ds(pl.multiple_of((second_at[half] + e) % SIDE * GROUP, GROUP), GROUP)

    def opp_copy(half, side, e):
        i = 4 * half + 2 * side + (e in (1, 0))
        return remote(
            prod.at[half * SIDE + 2, rows_of(half, e), :],
            opp_in.at[i], opp_send.at[i], opp_recv.at[i],
            along(half, 1 if side == 0 else 3),
        )

    def side_copy(half, side, e):
        i = 8 * half + 4 * side + e
        return remote(
            prod.at[half * SIDE + (1 if side == 0 else 3), rows_of(half, e), :],
            side_in.at[2 * half + side, rows_of(half, e), :],
            side_send.at[i], side_recv.at[i],
            along(half, 1 if side == 0 else 3),
        )

    def multiply(i):
        half, rel = order[i]
        at = half * SIDE + rel
        shared_loads[i].wait()
        if i + 3 < 8:
            shared_loads[i + 3].start()
        prod[at] = jnp.dot(panel[...], shared[at], preferred_element_type=F32)

    def relay(half, side, e):
        opp_copy(half, side, e).wait_recv()
        prod[half * SIDE + (1 if side == 0 else 3), rows_of(half, e), :] += opp_in[
            4 * half + 2 * side + (e in (1, 0))
        ]
        side_copy(half, side, e).start()

    multiply(0)
    pl.semaphore_wait(barrier, 13)
    for half in range(2):
        if half:
            multiply(1)
        for side, e in ((0, 2), (1, 3), (0, 1), (1, 0)):
            opp_copy(half, side, e).start()
    gram_part[0] = lax.dot_general(
        panel[own_rows, :],
        panel[...],
        (((1,), (1,)), ((), ())),
        preferred_element_type=F32,
    )
    for copy in g1:
        copy.start()
    for i, side, e in ((2, 0, 3), (3, 0, 3), (4, 1, 2), (5, 1, 2)):
        multiply(i)
        side_copy(order[i][0], side, e).start()
    for load in loads[3:]:
        load.start()
    for copy in g1:
        copy.wait_recv()
    gram_part[1] = gram_part[0] + gram_in[0] + gram_in[1] + gram_in[2]
    for copy in g2:
        copy.start()

    for half in range(2):
        relay(half, 0, 2)
        relay(half, 1, 3)
    multiply(6)
    multiply(7)
    for half in range(2):
        relay(half, 0, 1)
        side_copy(half, 1, 1).start()
    for half in range(2):
        relay(half, 1, 0)
        side_copy(half, 0, 0).start()

    for copy in g2:
        copy.wait_recv()
    gram_part[2] = gram_part[1] + gram_in[3] + gram_in[4] + gram_in[5]
    for copy in g3:
        copy.start()
    gram_full[own_rows, :] = gram_part[2]

    def group_copy(half, e):
        i = 3 * half + e - 1
        return remote(
            total.at[half, rows_of(half, e), :], group_in.at[i], group_send.at[i], group_recv.at[i],
            across(half, e),
        )

    def finish(half, e):
        side_copy(half, 0, e).wait_recv()
        side_copy(half, 1, e).wait_recv()
        here = rows_of(half, e)
        total[half, here, :] = (
            prod[half * SIDE, here, :] + side_in[2 * half, here, :] + side_in[2 * half + 1, here, :]
        )
        if e:
            group_copy(half, e).start()

    for e in (2, 3):
        for half in range(2):
            finish(half, e)

    for load in loads[3:]:
        load.wait()
    prior_t[...] = prior[...].T
    for half in range(2):
        own = rows_of(half, 0)
        full[half * SIDE + first_at[half], own, :] = jnp.dot(
            prior_t[own, :], prior_cols[half], precision=HI, preferred_element_type=F32
        )
    for e in (1, 0):
        for half in range(2):
            finish(half, e)
    z[...] = jnp.dot(prior_t[...], prior[...], precision=HI, preferred_element_type=F32)

    def own_copy(half, d):
        i = 3 * half + d - 1
        here = full.at[half * SIDE + first_at[half], rows_of(half, 0), :]
        return remote(here, here, gs_send.at[i], gs_recv.at[i], across(half, d))

    def chunk_copy(half, d, side):
        i = 8 * half + 2 * d + side
        here = full.at[half * SIDE + first_at[half], rows_of(half, SIDE - d), :]
        return remote(here, here, gp_send.at[i], gp_recv.at[i], along(half, 1 if side == 0 else 3))

    def forward_copy(half, d, side):
        i = 8 * half + 2 * d + side
        start = (second_at[half] + SIDE - d) % SIDE * GROUP + side * (GROUP // 2)
        here = full.at[
            half * SIDE + (first_at[half] + (3 if side == 0 else 1)) % SIDE,
            pl.ds(pl.multiple_of(start, GROUP // 2), GROUP // 2),
            :,
        ]
        return remote(here, here, gf_send.at[i], gf_recv.at[i], along(half, 1 if side == 0 else 3))

    for half in range(2):
        for e in (3, 1, 2):
            group_copy(half, e).wait_recv()
        own = rows_of(half, 0)
        full[half * SIDE + first_at[half], own, :] += (
            total[half, own, :]
            + group_in[3 * half]
            + group_in[3 * half + 1]
            + group_in[3 * half + 2]
        )
        for d in (2, 1, 3):
            own_copy(half, d).start()
    for half in range(2):
        chunk_copy(half, 0, 0).start()
        chunk_copy(half, 0, 1).start()

    for copy in g3:
        copy.wait_recv()
    z[...] += gram_full[...]
    pieces = factor_pieces(z, upper, inverse)

    def advance(count):
        for _ in range(count):
            next(pieces, None)

    advance(8)
    for d in (1, 3):
        for half in range(2):
            own_copy(half, d).wait_recv()
            chunk_copy(half, d, 0).start()
            chunk_copy(half, d, 1).start()
    advance(3)
    for half in range(2):
        own_copy(half, 2).wait_recv()
        chunk_copy(half, 2, 0).start()
        chunk_copy(half, 2, 1).start()
    for d in (0, 1, 3, 2):
        advance(3)
        for half in range(2):
            for side in range(2):
                chunk_copy(half, d, side).wait_recv()
                forward_copy(half, d, side).start()
    for _ in pieces:
        pass

    for d in (0, 1, 3, 2):
        for half in range(2):
            for side in range(2):
                forward_copy(half, d, side).wait_recv()

    for copy in g1 + g2 + g3:
        copy.wait_send()
    for half in range(2):
        for side, e in ((0, 2), (1, 3), (0, 1), (1, 0)):
            opp_copy(half, side, e).wait_send()
        for side in range(2):
            for e in range(SIDE):
                side_copy(half, side, e).wait_send()
                chunk_copy(half, e, side).wait_send()
                forward_copy(half, e, side).wait_send()
        for d in (1, 2, 3):
            group_copy(half, d).wait_send()
            own_copy(half, d).wait_send()


def apply_kernel(upper, inverse, full, upper_hbm, out_hbm, out, sem):
    upper_copy = pltpu.make_async_copy(upper, upper_hbm, sem.at[8])
    upper_copy.start()
    w1, w2 = split2(inverse[...])
    weights = jnp.concatenate([w1, w1, w2], axis=1)
    copies = []
    for i in range(8):
        a1, a2 = split2(full[i])
        out[i] = jnp.dot(
            weights, jnp.concatenate([a1, a2, a1], axis=0), preferred_element_type=F32
        )
        copies.append(
            pltpu.make_async_copy(out.at[i], out_hbm.at[:, pl.ds(i * CHUNK, CHUNK)], sem.at[i])
        )
        copies[-1].start()
    upper_copy.wait()
    for copy in copies:
        copy.wait()


def per_device(coefficients, arc_pairs, live_rows, shared_rows, prior_panel, prior_shared):
    rows, columns = shared_rows.shape
    hbm = pl.BlockSpec(memory_space=pltpu.HBM)
    vmem = pl.BlockSpec(memory_space=pltpu.VMEM)
    dma = pltpu.SemaphoreType.DMA
    upper, inverse, full = pl.pallas_call(
        kernel,
        out_shape=[
            pltpu.VMEM((PANEL, PANEL), F32),
            pltpu.VMEM((PANEL, PANEL), F32),
            pltpu.VMEM((8, PANEL, CHUNK), F32),
        ],
        in_specs=[hbm] * 6,
        out_specs=[vmem] * 3,
        scratch_shapes=[
            pltpu.VMEM(coefficients.shape, BF16),
            pltpu.VMEM(arc_pairs.shape, jnp.int32),
            pltpu.SMEM(live_rows.shape, jnp.int32),
            pltpu.VMEM((PANEL, PANEL), F32),
            pltpu.VMEM((PANEL, PANEL), F32),
            pltpu.VMEM((2, PANEL, CHUNK), F32),
            pltpu.VMEM((PANEL, rows), BF16),
            pltpu.VMEM((8, rows, CHUNK), BF16),
            pltpu.VMEM((8, PANEL, CHUNK), F32),
            pltpu.VMEM((8, GROUP, CHUNK), F32),
            pltpu.VMEM((4, PANEL, CHUNK), F32),
            pltpu.VMEM((2, PANEL, CHUNK), F32),
            pltpu.VMEM((6, GROUP, CHUNK), F32),
            pltpu.VMEM((3, 32, PANEL), F32),
            pltpu.VMEM((6, 32, PANEL), F32),
            pltpu.VMEM((PANEL, PANEL), F32),
            pltpu.VMEM((PANEL, PANEL), F32),
            dma((6,)), dma((8,)),
            dma((8,)), dma((8,)), dma((16,)), dma((16,)), dma((6,)), dma((6,)),
            dma((6,)), dma((6,)), dma((16,)), dma((16,)), dma((16,)), dma((16,)),
            dma((3,)), dma((3,)), dma((3,)), dma((3,)), dma((7,)), dma((7,)),
        ],
        compiler_params=pltpu.CompilerParams(
            collective_id=0, has_side_effects=True, vmem_limit_bytes=60 << 20
        ),
    )(coefficients, arc_pairs, live_rows, shared_rows, prior_panel, prior_shared)
    return pl.pallas_call(
        apply_kernel,
        out_shape=[
            jax.ShapeDtypeStruct((PANEL, PANEL), F32),
            jax.ShapeDtypeStruct((PANEL, columns), F32),
        ],
        in_specs=[vmem] * 3,
        out_specs=[hbm] * 2,
        scratch_shapes=[pltpu.VMEM((8, PANEL, CHUNK), F32), dma((9,))],
        compiler_params=pltpu.CompilerParams(vmem_limit_bytes=16 << 20),
    )(upper, inverse, full)


def solution(mesh):
    in_specs = (P(None, "dp"), P(None, "dp"), P("dp"), P("dp", "col"), P(), P(None, "col"))
    out_specs = (P(), P(None, "col"))
    return jax.shard_map(
        per_device, mesh=mesh, in_specs=in_specs, out_specs=out_specs, check_vma=False
    )
```

```python
import jax
import jax.numpy as jnp
from jax import lax
from jax.experimental import pallas as pl
from jax.experimental.pallas import tpu as pltpu
from jax.sharding import PartitionSpec as P

ARCS = 32
F32 = jnp.float32
BF16 = jnp.bfloat16
HI = lax.Precision.HIGHEST
MESH = pl.DeviceIdType.MESH
SIDE = 4
PANEL = 256
CHUNK = 256
GROUP = PANEL // SIDE
HALF = PANEL // 2


def split3(a):
    first = a.astype(BF16)
    rest = a - first.astype(F32)
    second = rest.astype(BF16)
    return first, second, (rest - second.astype(F32)).astype(BF16)


def product(x, y):
    x1, x2, x3 = split3(x)
    y1, y2, y3 = split3(y)
    return jnp.dot(
        jnp.concatenate([x1, x1, x2, x2, x1, x3], axis=1),
        jnp.concatenate([y1, y2, y1, y2, y3, y1], axis=0),
        preferred_element_type=F32,
    )


def factor_pieces(z_ref, upper_ref, inverse_ref):
    n = 64
    sub = lax.broadcasted_iota(jnp.int32, (8, 2 * n), 0)
    for k in range(PANEL // n):
        low, high = n * k, n * k + n
        lane = lax.broadcasted_iota(jnp.int32, (n, n), 1)
        row = lax.broadcasted_iota(jnp.int32, (n, n), 0)
        z = jnp.concatenate([z_ref[low:high, low:high], (lane == row).astype(F32)], axis=1)
        done = []
        for b in range(n // 8):
            m = n - 8 * b
            cols = [jnp.broadcast_to(z[:, 8 * b + j : 8 * b + j + 1], (m, 2 * n)) for j in range(8)]
            rows = lax.broadcasted_iota(jnp.int32, (m, 2 * n), 0)
            pivots = jnp.zeros((8, 2 * n), F32)
            for j in range(8):
                pivot = jnp.broadcast_to(cols[j][j : j + 1, :], (8, 2 * n))
                inverse = 1.0 / pivot
                pivots = jnp.where(sub == j, pivot, pivots)
                scale = jnp.where(
                    rows > j, cols[j] * jnp.broadcast_to(inverse[0:1], (m, 2 * n)), 0.0
                )
                for i in range(j + 1, 8):
                    cols[i] = cols[i] - scale * jnp.broadcast_to(cols[i][j : j + 1, :], (m, 2 * n))
                z = z - scale * jnp.broadcast_to(z[j : j + 1, :], (m, 2 * n))
            done.append(z[:8] * lax.rsqrt(pivots))
            z = z[8:]
            if b % 2 and b < 7:
                yield
        v = jnp.concatenate(done, axis=0)[:, n:]
        t = product(v, z_ref[low:high, :])
        lane = lax.broadcasted_iota(jnp.int32, (n, PANEL), 1)
        row = lax.broadcasted_iota(jnp.int32, (n, PANEL), 0)
        upper_ref[low:high, :] = jnp.where(lane >= low + row, t, 0.0)
        parts = [t[:, :low]] if k else []
        parts.append(v)
        if high < PANEL:
            parts.append(jnp.zeros((n, PANEL - high), F32))
        inverse = jnp.concatenate(parts, axis=1)
        inverse_ref[low:high, :] = inverse
        yield
        if high < PANEL:
            update = product(t[:, high:].T, jnp.where(lane < high, inverse, t))
            lane = lax.broadcasted_iota(jnp.int32, (PANEL - high, PANEL), 1)
            old = jnp.where((lane >= low) & (lane < high), 0.0, z_ref[high:, :])
            z_ref[high:, :] = old - update
            yield


def split2(a):
    first = a.astype(BF16)
    return first, (a - first.astype(F32)).astype(BF16)


def kernel(
    coef_hbm, arcs_hbm, live_hbm, shared_hbm, prior_hbm, prior_shared_hbm,
    upper, inverse, full,
    coef, arcs, live, prior, prior_t, prior_cols, panel, shared, prod, opp_in, side_in, total, group_in,
    gram_part, gram_in, gram_full, z,
    small_sem, shared_sem,
    opp_send, opp_recv, side_send, side_recv, group_send, group_recv,
    gs_send, gs_recv, gp_send, gp_recv, gf_send, gf_recv,
    g1_send, g1_recv, g2_send, g2_recv, g3_send, g3_recv,
):
    dp, col = lax.axis_index("dp"), lax.axis_index("col")
    x, z_at = dp // SIDE, dp % SIDE
    y, core = col // 2, col % 2

    def device(dx=0, dz=0, dy=0, dc=0):
        return (
            (x + dx) % SIDE * SIDE + (z_at + dz) % SIDE,
            (y + dy) % SIDE * 2 + (core + dc) % 2,
        )

    def along(half, d):
        return device(dx=d) if half == 0 else device(dz=d)

    def across(half, d):
        return device(dz=d) if half == 0 else device(dx=d)

    first_at = (x, z_at)
    second_at = (z_at, x)

    barrier = pltpu.get_barrier_semaphore()
    for d in (1, 2, 3):
        pl.semaphore_signal(barrier, inc=1, device_id=device(dx=d), device_id_type=MESH)
        pl.semaphore_signal(barrier, inc=1, device_id=device(dz=d), device_id_type=MESH)
    for dy in range(SIDE):
        for dc in range(2):
            if dy or dc:
                pl.semaphore_signal(
                    barrier, inc=1, device_id=device(dy=dy, dc=dc), device_id_type=MESH
                )

    loads = [
        pltpu.make_async_copy(arcs_hbm, arcs, small_sem.at[0]),
        pltpu.make_async_copy(coef_hbm, coef, small_sem.at[1]),
        pltpu.make_async_copy(live_hbm, live, small_sem.at[2]),
        pltpu.make_async_copy(prior_hbm, prior, small_sem.at[3]),
    ]
    for half in range(2):
        start = pl.multiple_of((half * SIDE + first_at[half]) * CHUNK, CHUNK)
        loads.append(
            pltpu.make_async_copy(
                prior_shared_hbm.at[:, pl.ds(start, CHUNK)],
                prior_cols.at[half],
                small_sem.at[4 + half],
            )
        )
    order = [(half, rel) for rel in (2, 1, 3, 0) for half in range(2)]
    shared_loads = []
    for half, rel in order:
        start = pl.multiple_of((half * SIDE + (first_at[half] + rel) % SIDE) * CHUNK, CHUNK)
        shared_loads.append(
            pltpu.make_async_copy(
                shared_hbm.at[:, pl.ds(start, CHUNK)],
                shared.at[half * SIDE + rel],
                shared_sem.at[half * SIDE + rel],
            )
        )
    for load in loads[:3]:
        load.start()
    shared_loads[0].start()

    rows = arcs.shape[1]
    for load in loads[:3]:
        load.wait()
    live_count = live[0]
    shared_loads[1].start()
    shared_loads[2].start()
    step = 512

    def build(i, carry):
        at = pl.ds(pl.multiple_of(i * step, step), step)
        pair = arcs[:, at]
        inside = i * step + lax.broadcasted_iota(jnp.int32, (1, step), 1) < live_count
        pair = jnp.where(inside, pair, -1).astype(F32)
        one = jnp.broadcast_to(pair[0:1], (16, step)).astype(BF16)
        two = jnp.broadcast_to(pair[1:2], (16, step)).astype(BF16)
        values = coef[:, at]
        first_values = jnp.concatenate([values[:8], values[:8]], axis=0)
        second_values = jnp.concatenate([values[8:], values[8:]], axis=0)
        odd = (lax.broadcasted_iota(jnp.int32, (16, step), 0) // 8).astype(F32)
        for a in range(0, ARCS, 2):
            arc = (odd + a).astype(BF16)
            panel[8 * a : 8 * a + 16, at] = jnp.where(
                one == arc, first_values, jnp.where(two == arc, second_values, jnp.zeros((), BF16))
            )
        return carry

    lax.fori_loop(0, rows // step, build, 0)
    shared_loads[3].start()

    own_rows = pl.ds(pl.multiple_of(col * 32, 32), 32)

    def remote(src, dst, send, recv, to):
        return pltpu.make_async_remote_copy(
            src_ref=src, dst_ref=dst, send_sem=send, recv_sem=recv, device_id=to, device_id_type=MESH
        )

    def gram_axis(d, second):
        if second:
            return device(dx=d * core, dz=d * (1 - core))
        return device(dx=d * (1 - core), dz=d * core)

    g1 = [
        remote(gram_part.at[0], gram_in.at[d - 1], g1_send.at[d - 1], g1_recv.at[d - 1], gram_axis(d, False))
        for d in (1, 2, 3)
    ]
    g2 = [
        remote(gram_part.at[1], gram_in.at[2 + d], g2_send.at[d - 1], g2_recv.at[d - 1], gram_axis(d, True))
        for d in (1, 2, 3)
    ]
    g3 = []
    for dy in range(SIDE):
        for dc in range(2):
            if dy or dc:
                i = 2 * dy + dc - 1
                g3.append(
                    remote(
                        gram_part.at[2], gram_full.at[own_rows, :], g3_send.at[i], g3_recv.at[i],
                        device(dy=dy, dc=dc),
                    )
                )
    def rows_of(half, e):
        return pl.ds(pl.multiple_of((second_at[half] + e) % SIDE * GROUP, GROUP), GROUP)

    def opp_copy(half, side, e):
        i = 4 * half + 2 * side + (e in (1, 0))
        return remote(
            prod.at[half * SIDE + 2, rows_of(half, e), :],
            opp_in.at[i], opp_send.at[i], opp_recv.at[i],
            along(half, 1 if side == 0 else 3),
        )

    def side_copy(half, side, e):
        i = 8 * half + 4 * side + e
        return remote(
            prod.at[half * SIDE + (1 if side == 0 else 3), rows_of(half, e), :],
            side_in.at[2 * half + side, rows_of(half, e), :],
            side_send.at[i], side_recv.at[i],
            along(half, 1 if side == 0 else 3),
        )

    def multiply(i):
        half, rel = order[i]
        at = half * SIDE + rel
        shared_loads[i].wait()
        if 4 <= i + 4 < 8:
            shared_loads[i + 4].start()
        prod[at] = jnp.dot(panel[...], shared[at], preferred_element_type=F32)

    def relay(half, side, e):
        opp_copy(half, side, e).wait_recv()
        prod[half * SIDE + (1 if side == 0 else 3), rows_of(half, e), :] += opp_in[
            4 * half + 2 * side + (e in (1, 0))
        ]
        side_copy(half, side, e).start()

    gram_part[0] = lax.dot_general(
        panel[own_rows, :],
        panel[...],
        (((1,), (1,)), ((), ())),
        preferred_element_type=F32,
    )
    multiply(0)
    pl.semaphore_wait(barrier, 13)
    for copy in g1:
        copy.start()
    for half in range(2):
        if half:
            multiply(1)
        opp_copy(half, 0, 2).start()
        opp_copy(half, 1, 3).start()
    for half in range(2):
        opp_copy(half, 0, 1).start()
        opp_copy(half, 1, 0).start()
    for i, side, e in ((2, 0, 3), (3, 0, 3), (4, 1, 2), (5, 1, 2)):
        multiply(i)
        side_copy(order[i][0], side, e).start()
    for load in loads[3:]:
        load.start()

    for copy in g1:
        copy.wait_recv()
    gram_part[1] = gram_part[0] + gram_in[0] + gram_in[1] + gram_in[2]
    for copy in g2:
        copy.start()
    for half in range(2):
        relay(half, 0, 2)
        relay(half, 1, 3)
    multiply(6)
    multiply(7)
    for half in range(2):
        relay(half, 0, 1)
        side_copy(half, 1, 1).start()
    for half in range(2):
        relay(half, 1, 0)
        side_copy(half, 0, 0).start()


    for load in loads[3:]:
        load.wait()
    prior_t[...] = prior[...].T
    for half in range(2):
        own = rows_of(half, 0)
        full[half * SIDE + first_at[half], own, :] = jnp.dot(
            prior_t[own, :], prior_cols[half], precision=HI, preferred_element_type=F32
        )
    def group_copy(half, e):
        i = 3 * half + e - 1
        return remote(
            total.at[half, rows_of(half, e), :], group_in.at[i], group_send.at[i], group_recv.at[i],
            across(half, e),
        )

    def finish(half, e):
        side_copy(half, 0, e).wait_recv()
        side_copy(half, 1, e).wait_recv()
        here = rows_of(half, e)
        total[half, here, :] = (
            prod[half * SIDE, here, :] + side_in[2 * half, here, :] + side_in[2 * half + 1, here, :]
        )
        if e:
            group_copy(half, e).start()

    for e in (2, 3):
        for half in range(2):
            finish(half, e)

    for copy in g2:
        copy.wait_recv()
    gram_part[2] = gram_part[1] + gram_in[3] + gram_in[4] + gram_in[5]
    for copy in g3:
        copy.start()
    gram_full[own_rows, :] = gram_part[2]
    for e in (1, 0):
        for half in range(2):
            finish(half, e)
    for copy in g1 + g2:
        copy.wait_send()
    for half in range(2):
        for side, e in ((0, 2), (1, 3), (0, 1), (1, 0)):
            opp_copy(half, side, e).wait_send()
        for side in range(2):
            for e in range(SIDE):
                side_copy(half, side, e).wait_send()
    z[...] = jnp.dot(prior_t[...], prior[...], precision=HI, preferred_element_type=F32)

    def own_copy(half, d):
        i = 3 * half + d - 1
        here = full.at[half * SIDE + first_at[half], rows_of(half, 0), :]
        return remote(here, here, gs_send.at[i], gs_recv.at[i], across(half, d))

    def chunk_copy(half, d, side):
        i = 8 * half + 2 * d + side
        here = full.at[half * SIDE + first_at[half], rows_of(half, SIDE - d), :]
        return remote(here, here, gp_send.at[i], gp_recv.at[i], along(half, 1 if side == 0 else 3))

    def forward_copy(half, d, side):
        i = 8 * half + 2 * d + side
        start = (second_at[half] + SIDE - d) % SIDE * GROUP + side * (GROUP // 2)
        here = full.at[
            half * SIDE + (first_at[half] + (3 if side == 0 else 1)) % SIDE,
            pl.ds(pl.multiple_of(start, GROUP // 2), GROUP // 2),
            :,
        ]
        return remote(here, here, gf_send.at[i], gf_recv.at[i], along(half, 1 if side == 0 else 3))

    for half in range(2):
        for e in (3, 1, 2):
            group_copy(half, e).wait_recv()
        own = rows_of(half, 0)
        full[half * SIDE + first_at[half], own, :] += (
            total[half, own, :]
            + group_in[3 * half]
            + group_in[3 * half + 1]
            + group_in[3 * half + 2]
        )
        for d in (1, 3, 2):
            own_copy(half, d).start()
    for half in range(2):
        chunk_copy(half, 0, 0).start()
        chunk_copy(half, 0, 1).start()

    for copy in g3:
        copy.wait_recv()
    z[...] += gram_full[...]
    pieces = factor_pieces(z, upper, inverse)

    def advance(count):
        for _ in range(count):
            next(pieces, None)

    advance(8)
    for d in (1, 3):
        for half in range(2):
            own_copy(half, d).wait_recv()
            chunk_copy(half, d, 0).start()
            chunk_copy(half, d, 1).start()
    advance(3)
    for half in range(2):
        for d in (1, 2, 3):
            group_copy(half, d).wait_send()
    for copy in g3:
        copy.wait_send()
    for half in range(2):
        own_copy(half, 2).wait_recv()
        chunk_copy(half, 2, 0).start()
        chunk_copy(half, 2, 1).start()
    for d in (0, 1, 3, 2):
        advance(3)
        for half in range(2):
            for side in range(2):
                chunk_copy(half, d, side).wait_recv()
                forward_copy(half, d, side).start()
    for _ in pieces:
        pass
    for half in range(2):
        for d in (1, 2, 3):
            own_copy(half, d).wait_send()
        for side in range(2):
            for d in (0, 1, 3):
                chunk_copy(half, d, side).wait_send()

    for d in (0, 1, 3, 2):
        for half in range(2):
            for side in range(2):
                forward_copy(half, d, side).wait_recv()

    for half in range(2):
        for side in range(2):
            for d in range(SIDE):
                forward_copy(half, d, side).wait_send()
            chunk_copy(half, 2, side).wait_send()


def apply_kernel(upper, inverse, full, upper_hbm, out_hbm, out, sem):
    upper_copy = pltpu.make_async_copy(upper, upper_hbm, sem.at[8])
    upper_copy.start()
    w1, w2 = split2(inverse[...])
    weights = jnp.concatenate([w1, w1, w2], axis=1)
    copies = []
    for i in range(8):
        a1, a2 = split2(full[i])
        out[i] = jnp.dot(
            weights, jnp.concatenate([a1, a2, a1], axis=0), preferred_element_type=F32
        )
        copies.append(
            pltpu.make_async_copy(out.at[i], out_hbm.at[:, pl.ds(i * CHUNK, CHUNK)], sem.at[i])
        )
        copies[-1].start()
    upper_copy.wait()
    for copy in copies:
        copy.wait()


def per_device(coefficients, arc_pairs, live_rows, shared_rows, prior_panel, prior_shared):
    rows, columns = shared_rows.shape
    hbm = pl.BlockSpec(memory_space=pltpu.HBM)
    vmem = pl.BlockSpec(memory_space=pltpu.VMEM)
    dma = pltpu.SemaphoreType.DMA
    upper, inverse, full = pl.pallas_call(
        kernel,
        out_shape=[
            pltpu.VMEM((PANEL, PANEL), F32),
            pltpu.VMEM((PANEL, PANEL), F32),
            pltpu.VMEM((8, PANEL, CHUNK), F32),
        ],
        in_specs=[hbm] * 6,
        out_specs=[vmem] * 3,
        scratch_shapes=[
            pltpu.VMEM(coefficients.shape, BF16),
            pltpu.VMEM(arc_pairs.shape, jnp.int32),
            pltpu.SMEM(live_rows.shape, jnp.int32),
            pltpu.VMEM((PANEL, PANEL), F32),
            pltpu.VMEM((PANEL, PANEL), F32),
            pltpu.VMEM((2, PANEL, CHUNK), F32),
            pltpu.VMEM((PANEL, rows), BF16),
            pltpu.VMEM((8, rows, CHUNK), BF16),
            pltpu.VMEM((8, PANEL, CHUNK), F32),
            pltpu.VMEM((8, GROUP, CHUNK), F32),
            pltpu.VMEM((4, PANEL, CHUNK), F32),
            pltpu.VMEM((2, PANEL, CHUNK), F32),
            pltpu.VMEM((6, GROUP, CHUNK), F32),
            pltpu.VMEM((3, 32, PANEL), F32),
            pltpu.VMEM((6, 32, PANEL), F32),
            pltpu.VMEM((PANEL, PANEL), F32),
            pltpu.VMEM((PANEL, PANEL), F32),
            dma((6,)), dma((8,)),
            dma((8,)), dma((8,)), dma((16,)), dma((16,)), dma((6,)), dma((6,)),
            dma((6,)), dma((6,)), dma((16,)), dma((16,)), dma((16,)), dma((16,)),
            dma((3,)), dma((3,)), dma((3,)), dma((3,)), dma((7,)), dma((7,)),
        ],
        compiler_params=pltpu.CompilerParams(
            collective_id=0, has_side_effects=True, vmem_limit_bytes=60 << 20
        ),
    )(coefficients, arc_pairs, live_rows, shared_rows, prior_panel, prior_shared)
    return pl.pallas_call(
        apply_kernel,
        out_shape=[
            jax.ShapeDtypeStruct((PANEL, PANEL), F32),
            jax.ShapeDtypeStruct((PANEL, columns), F32),
        ],
        in_specs=[vmem] * 3,
        out_specs=[hbm] * 2,
        scratch_shapes=[pltpu.VMEM((8, PANEL, CHUNK), F32), dma((9,))],
        compiler_params=pltpu.CompilerParams(vmem_limit_bytes=16 << 20),
    )(upper, inverse, full)


def solution(mesh):
    in_specs = (P(None, "dp"), P(None, "dp"), P("dp"), P("dp", "col"), P(), P(None, "col"))
    out_specs = (P(), P(None, "col"))
    return jax.shard_map(
        per_device, mesh=mesh, in_specs=in_specs, out_specs=out_specs, check_vma=False
    )
```
